32 devices in a mesh: groups: 2 (over y), expert: 4 (over z), dp: 4 (over x, core).
Axes of the slice: x: 2, y: 2, z: 4, core: 2. Of those that a mesh axis runs over, the one named last changes fastest.
Arguments:
- tokens: bfloat16 [1024, 4096], P(('groups', 'expert'), 'dp'), parts along dimension 0, may hold values from -6 to 6
- routes: int32 [1024, 4], P(('groups', 'expert')), parts along dimension 0, may hold values from 0 to 7, all different within a row; in each aligned block of 128 rows (0 to 127, 128 to 255, ...) at most 128 rows name the same one
- gates: float32 [1024, 4], P(('groups', 'expert')), parts along dimension 0, may hold values from 0.05 to 1
- w_in: bfloat16 [4096, 1024], P(('dp', 'expert')), may hold values from -0.09375 to 0.09375
- w_out: bfloat16 [4096, 1024], P(('dp', 'expert')), may hold values from -0.1875 to 0.1875
- w_first: bfloat16 [8, 1024, 1024], P('expert', None, 'dp'), may hold values from -0.1875 to 0.1875
- w_second: bfloat16 [8, 1024, 1024], P('expert', 'dp'), may hold values from -0.1875 to 0.1875
- out_grad: bfloat16 [1024, 4096], P(('groups', 'expert'), 'dp'), parts along dimension 0, may hold values from -6 to 6
Outputs:
- mixed: bfloat16 [1024, 4096], P(('groups', 'expert'), 'dp'), parts along dimension 0
- grad_tokens: bfloat16 [1024, 4096], P(('groups', 'expert'), 'dp'), parts along dimension 0
- grad_w_in: float32 [8192, 1024], P(('groups', 'dp', 'expert')), parts along dimension 0
- grad_w_out: float32 [8192, 1024], P(('groups', 'dp', 'expert')), parts along dimension 0
- grad_first: bfloat16 [16, 1024, 1024], P(('groups', 'expert'), None, 'dp'), parts along dimension 0
- grad_second: bfloat16 [16, 1024, 1024], P(('groups', 'expert'), 'dp'), parts along dimension 0
The draws below stay inside these ranges and needn't reach their ends.
There are 2 independent parts, one for each index of `groups`. The reference program is written for one: setup_inputs(seed, part) draws one part's arguments, and reference() takes and returns one part's arrays. A program takes and returns all parts, laid end to end along the dimension named above; an argument that names none is the same for every part. Nothing has to cross between parts.
Inputs may be any that keep to these rules, and one draw needn't show every extreme that they name: `routes`: each row names 4 different experts. Within each aligned block of 128 rows no expert is named by more than 128 rows, a bound that some block reaches.
All inputs are finite; a program needn't handle non-finite values.
Results may differ from the reference program's by a relative error of at most 0.025.
Values may be sent and summed in bfloat16 or wider, within the bound.
A program may use at most 64 MiB of HBM per device.

```python
import math
import jax
import jax.numpy as jnp
import numpy as np
from jax import lax

D = 4096
LATENT = 1024
FF = 1024
TOPK = 4
TOK_DEV = 128
EXPERTS = 8
CAP = 128
TOKENS = 512
N_EXPERT = 4
N_DP = 4


def block_scale(own_key, extent, split, least, high):
    level, own = 1.0, jax.random.fold_in(own_key, 6)
    for dim, blocks in split:
        draws = jnp.exp(jax.random.uniform(jax.random.fold_in(own, dim), (blocks,), jnp.float32, least / len(split), high / len(split)))
        level = level * jnp.repeat(draws, extent[dim] // blocks).reshape([-1 if axis == dim else 1 for axis in range(len(extent))])
    return level


def deal_out(own_key, own, number, rows, count, top, most, lean):
    order = jax.random.permutation(own_key, count)
    heavy_load, usual = load_shares(count, rows * top, most, lean, True), load_shares(count, rows * top, most, lean, False)
    places = jnp.arange(count)

    def named(tallies, turn):
        used = int((tallies > 0).sum())
        fixed = max(1, used // 4)
        passed = fixed + (places - fixed + turn * (used - fixed)) % max(1, count - fixed)
        return jnp.zeros((count,), jnp.int32).at[order[jnp.where(places < fixed, places, passed)]].set(jnp.asarray(tallies, jnp.int32))

    tallies = jnp.where(number % 4 == 0, named(heavy_load, number // 4), named(usual, number - number // 4 - 1))
    mixed = jax.random.permutation(jax.random.fold_in(own, 3), count)
    donor, receiver = mixed[0:count // 2 * 2:2], mixed[1:count // 2 * 2:2]
    margin = jnp.minimum(tallies[donor] - 1, most - tallies[receiver]) // 2
    margin = jnp.where((donor == order[0]) | (receiver == order[0]) | (tallies[receiver] == 0), 0, jnp.maximum(margin, 0))
    passed = jax.random.randint(jax.random.fold_in(own, 4), (count // 2,), 0, 1 << 20) % (margin + 1)
    tallies = tallies.at[donor].add(-passed).at[receiver].add(passed)
    items = jnp.searchsorted(jnp.cumsum(tallies), jnp.arange(rows * top), side="right").astype(jnp.int32)
    grid = items.reshape(top, rows).T
    grid = grid[jax.random.permutation(jax.random.fold_in(own, 1), rows)]
    turn = jax.random.randint(jax.random.fold_in(own, 2), (rows, 1), 0, top)
    return jnp.take_along_axis(grid, (jnp.arange(top)[None, :] + turn) % top, axis=1)


def load_shares(amount, total, most, lean, full):
    portions = [(1 << 20) // math.isqrt(standing ** lean) + 1 for standing in range(1, amount + 1)]
    largest = most if full else min(most, max(-(-total // amount), total * portions[0] // sum(portions)))
    least = 1 if total - largest >= amount - 1 else 0
    given, surplus = [largest] + [least] * (amount - 1), total - largest - least * (amount - 1)
    while surplus > 0:
        candidates = [i for i in range(1, amount) if given[i] < largest] or [i for i in range(1, amount) if given[i] < most]
        pool, left = sum([portions[i] for i in candidates]), surplus
        for i in candidates:
            addition = min(most - given[i], max(1, left * portions[i] // pool), surplus)
            given[i] = given[i] + addition
            surplus = surplus - addition
    return np.array(given)


def scatter_about(own_key, extent, deviation, limit, cuts=(), held_as=jnp.bfloat16):
    factor_of = block_scale(own_key, extent, cuts, -0.22, 0.18) if cuts else 1.0
    entries = jax.random.normal(own_key, extent, jnp.float32) * deviation * factor_of
    return jnp.minimum(jnp.maximum(entries, -limit), limit).astype(held_as)


def setup_inputs(seed: int = 0, part: int = 0) -> dict:
    splits = jax.random.split(jax.random.key(seed), 9)
    part_splits = jax.random.split(jax.random.fold_in(splits[8], part), 9)
    tokens = scatter_about(part_splits[0], (TOKENS, D), 1.0, 6.0, ((0, 4), (1, 4)))
    routes_keys = jax.random.split(jax.random.fold_in(part_splits[1], 1), TOKENS // TOK_DEV)
    routes_turns = jax.random.permutation(jax.random.fold_in(part_splits[1], 3), TOKENS // TOK_DEV)
    routes = jax.vmap(lambda own, number: deal_out(jax.random.fold_in(part_splits[1], 2), own, number, TOK_DEV, EXPERTS, TOPK, CAP, 1))(routes_keys, routes_turns).reshape((TOKENS, TOPK))
    gates = jnp.clip(jnp.exp(math.log(1.0) - 2.9957323 * jax.random.uniform(part_splits[2], (TOKENS, TOPK), jnp.float32) ** block_scale(part_splits[2], (TOKENS, TOPK), ((0, 4),), -0.2, 0.2)), 0.05, 1.0)
    w_in = scatter_about(splits[3], (D, LATENT), D ** -0.5, 0.09375, ((0, 16),))
    w_out = scatter_about(splits[4], (D, LATENT), LATENT ** -0.5, 0.1875, ((0, 16),))
    w_first = scatter_about(splits[5], (EXPERTS, LATENT, FF), LATENT ** -0.5, 0.1875, ((0, 4), (2, 4)))
    w_second = scatter_about(splits[6], (EXPERTS, FF, LATENT), FF ** -0.5, 0.1875, ((0, 4), (1, 4)))
    out_grad = scatter_about(part_splits[7], (TOKENS, D), 1.0, 6.0, ((0, 4), (1, 4)))
    return dict(tokens=tokens, routes=routes, gates=gates, w_in=w_in, w_out=w_out, w_first=w_first, w_second=w_second, out_grad=out_grad)


def expert_forward(operands):
    inputs, first, second = operands
    before = jnp.dot(inputs, first, preferred_element_type=jnp.float32)
    hidden = jnp.square(jax.nn.relu(before)).astype(jnp.bfloat16)
    parts = jnp.einsum('rdh,dhl->rdl', hidden.reshape(inputs.shape[0], N_DP, -1).astype(jnp.float32), second.reshape(N_DP, -1, second.shape[1]).astype(jnp.float32))
    parts = lax.optimization_barrier(parts.astype(jnp.bfloat16))
    return jnp.sum(parts.astype(jnp.float32), axis=1)


def expert_backward(operands):
    inputs, grads, first, second = operands
    before = jnp.dot(inputs, first, preferred_element_type=jnp.float32)
    hidden = jnp.square(jax.nn.relu(before)).astype(jnp.bfloat16)
    hidden_grad = jnp.dot(grads, second.T, preferred_element_type=jnp.float32)
    before_grad = (hidden_grad * 2.0 * jax.nn.relu(before)).astype(jnp.bfloat16)
    grad_second = jnp.dot(hidden.T, grads, preferred_element_type=jnp.float32).astype(jnp.bfloat16)
    grad_first = jnp.dot(inputs.T, before_grad, preferred_element_type=jnp.float32).astype(jnp.bfloat16)
    parts = jnp.einsum('rdh,ldh->rdl', before_grad.reshape(inputs.shape[0], N_DP, -1).astype(jnp.float32), first.reshape(first.shape[0], N_DP, -1).astype(jnp.float32))
    parts = lax.optimization_barrier(parts.astype(jnp.bfloat16))
    return grad_first, grad_second, jnp.sum(parts.astype(jnp.float32), axis=1)


def weight_block(total, block):
    token_block, dy_block, gin_block, lat_block = block
    term = jnp.concatenate([jnp.dot(token_block.T, gin_block, preferred_element_type=jnp.float32), jnp.dot(dy_block.T, lat_block, preferred_element_type=jnp.float32)], axis=1)
    term = lax.optimization_barrier(term.astype(jnp.bfloat16))
    return total + term.astype(jnp.float32), None


def reference(tokens, routes, gates, w_in, w_out, w_first, w_second, out_grad):
    latent = jnp.dot(tokens, w_in, preferred_element_type=jnp.float32).astype(jnp.bfloat16)
    flat = routes.reshape(-1).astype(jnp.int32)
    onehot = (flat[:, None] == jnp.arange(EXPERTS, dtype=jnp.int32)[None, :]).astype(jnp.int32)
    blocked = onehot.reshape(N_EXPERT, TOK_DEV * TOPK, EXPERTS)
    slot = jnp.sum(blocked * (jnp.cumsum(blocked, axis=1) - 1), axis=2).reshape(-1)
    source = jnp.arange(TOKENS * TOPK, dtype=jnp.int32) // (TOK_DEV * TOPK)
    dest = (flat * (N_EXPERT * CAP) + source * CAP + slot).astype(jnp.int32)
    total_rows = EXPERTS * N_EXPERT * CAP
    expert_input = jnp.zeros((total_rows, LATENT), jnp.bfloat16).at[dest].set(jnp.repeat(latent, TOPK, axis=0))
    expert_input = expert_input.reshape(EXPERTS, N_EXPERT * CAP, LATENT)
    outputs = lax.map(expert_forward, (expert_input, w_first, w_second))
    route_out = outputs.reshape(total_rows, LATENT)[dest]
    weights = gates.reshape(-1, 1)
    lat_out = jnp.sum((weights * route_out).reshape(TOKENS, TOPK, LATENT), axis=1).astype(jnp.bfloat16)
    mixed = jnp.dot(lat_out, w_out.T, preferred_element_type=jnp.float32).astype(jnp.bfloat16)
    grad_latent = jnp.dot(out_grad, w_out, preferred_element_type=jnp.float32).astype(jnp.bfloat16)
    route_grad = (weights * jnp.repeat(grad_latent, TOPK, axis=0).astype(jnp.float32)).astype(jnp.bfloat16)
    expert_grad = jnp.zeros((total_rows, LATENT), jnp.bfloat16).at[dest].set(route_grad)
    expert_grad = expert_grad.reshape(EXPERTS, N_EXPERT * CAP, LATENT)
    grad_first, grad_second, back = lax.map(expert_backward, (expert_input, expert_grad, w_first, w_second))
    back_rows = back.reshape(total_rows, LATENT)[dest]
    grad_in = jnp.sum(back_rows.reshape(TOKENS, TOPK, LATENT), axis=1).astype(jnp.bfloat16)
    grad_tokens = jnp.dot(grad_in, w_in.T, preferred_element_type=jnp.float32).astype(jnp.bfloat16)
    blocks = (tokens.reshape(N_EXPERT, TOK_DEV, D), out_grad.reshape(N_EXPERT, TOK_DEV, D), grad_in.reshape(N_EXPERT, TOK_DEV, LATENT), lat_out.reshape(N_EXPERT, TOK_DEV, LATENT))
    sums, unused = lax.scan(weight_block, jnp.zeros((D, 2 * LATENT), jnp.float32), blocks)
    return mixed, grad_tokens, sums[:, :LATENT], sums[:, LATENT:], grad_first, grad_second
```

```python
import jax
import jax.numpy as jnp
from jax import lax
from jax.sharding import PartitionSpec as P


def body(tokens, routes, gates, w_in, w_out, w_first, w_second, out_grad):
    in_full, out_full = (
        lax.all_gather(w_in, "expert", axis=0, tiled=True),
        lax.all_gather(w_out, "expert", axis=0, tiled=True),
    )
    token_count = tokens.shape[0]
    top_count = routes.shape[1]
    expert_local = w_first.shape[0]
    expert_shards = lax.axis_size("expert")
    expert_total = expert_local * expert_shards
    latent_width = w_in.shape[1]
    capacity = min(token_count, max(2, 5 * token_count * top_count // (2 * expert_total)))
    flat = routes.reshape(-1)
    onehot = (flat[:, None] == jnp.arange(expert_total, dtype=jnp.int32)[None, :]).astype(jnp.int32)
    slot = jnp.sum(onehot * (jnp.cumsum(onehot, axis=0) - 1), axis=1)
    dest = flat * capacity + slot
    weights = gates.reshape(-1, 1)

    def dp_total(value):
        return lax.psum(value.astype(jnp.bfloat16), "dp").astype(jnp.float32)

    def pack(route_rows):
        buffer = (
            jnp.zeros((expert_total * capacity, route_rows.shape[1]), route_rows.dtype)
            .at[dest]
            .set(route_rows)
        )
        return buffer.reshape(expert_shards, expert_local, capacity, route_rows.shape[1])

    def send(route_rows):
        share = latent_width // lax.axis_size("dp")
        columns = lax.dynamic_slice_in_dim(route_rows, lax.axis_index("dp") * share, share, 1)
        moved = lax.all_to_all(pack(columns), "expert", split_axis=0, concat_axis=0, tiled=True)
        return lax.all_gather(moved, "dp", axis=3, tiled=True)

    def combine_rows(buffer, scale):
        returned = lax.all_to_all(buffer, "expert", split_axis=0, concat_axis=0, tiled=True)
        rows = returned.reshape(expert_total * capacity, latent_width)[dest].astype(jnp.float32)
        if scale is not None:
            rows = scale * rows
        summed = jnp.sum(rows.reshape(token_count, top_count, latent_width), axis=1)
        return dp_total(summed).astype(jnp.bfloat16)

    latent = dp_total(jnp.dot(tokens, in_full, preferred_element_type=jnp.float32)).astype(
        jnp.bfloat16
    )
    arrived = send(jnp.repeat(latent, top_count, axis=0))
    before = jnp.einsum("sjcl,jlh->sjch", arrived, w_first, preferred_element_type=jnp.float32)
    hidden = jnp.square(jax.nn.relu(before)).astype(jnp.bfloat16)
    partial_out = jnp.einsum(
        "sjch,jhl->sjcl", hidden, w_second, preferred_element_type=jnp.float32
    ).astype(jnp.bfloat16)
    lat_out = combine_rows(partial_out, weights)
    mixed = jnp.dot(lat_out, out_full.T, preferred_element_type=jnp.float32).astype(jnp.bfloat16)
    grad_latent = dp_total(jnp.dot(out_grad, out_full, preferred_element_type=jnp.float32)).astype(
        jnp.bfloat16
    )
    route_grad = (weights * jnp.repeat(grad_latent, top_count, axis=0).astype(jnp.float32)).astype(
        jnp.bfloat16
    )
    incoming = send(route_grad)
    hidden_grad = jnp.einsum(
        "sjcl,jhl->sjch", incoming, w_second, preferred_element_type=jnp.float32
    )
    before_grad = (hidden_grad * 2.0 * jax.nn.relu(before)).astype(jnp.bfloat16)
    grad_second = jnp.einsum(
        "sjch,sjcl->jhl", hidden, incoming, preferred_element_type=jnp.float32
    ).astype(jnp.bfloat16)
    grad_first = jnp.einsum(
        "sjcl,sjch->jlh", arrived, before_grad, preferred_element_type=jnp.float32
    ).astype(jnp.bfloat16)
    back_piece = jnp.einsum(
        "sjch,jlh->sjcl", before_grad, w_first, preferred_element_type=jnp.float32
    ).astype(jnp.bfloat16)
    grad_in = combine_rows(back_piece, None)
    grad_tokens = jnp.dot(grad_in, in_full.T, preferred_element_type=jnp.float32).astype(
        jnp.bfloat16
    )
    first_term = jnp.dot(tokens.T, grad_in, preferred_element_type=jnp.float32)
    second_term = jnp.dot(out_grad.T, lat_out, preferred_element_type=jnp.float32)
    sums = lax.psum_scatter(
        jnp.concatenate([first_term, second_term], axis=1).astype(jnp.bfloat16),
        "expert",
        scatter_dimension=0,
        tiled=True,
    ).astype(jnp.float32)
    return (
        mixed,
        grad_tokens,
        sums[:, :latent_width],
        sums[:, latent_width:],
        grad_first,
        grad_second,
    )


def dense_body(tokens, routes, gates, w_in, w_out, w_first, w_second, out_grad):
    bf16, f32 = jnp.bfloat16, jnp.float32
    shards = lax.axis_size("expert")
    local, latent_width, hidden_width = w_first.shape
    depth = w_in.shape[0]

    def dot(a, b, dims):
        return lax.dot_general(a, b, (dims, ((), ())), preferred_element_type=f32)

    def total(value):
        return lax.psum(value.astype(bf16), ("expert", "dp"))

    def to_columns(value):
        return lax.all_to_all(value, "expert", split_axis=1, concat_axis=0, tiled=True)

    def to_rows(value):
        return lax.all_to_all(value, "expert", split_axis=0, concat_axis=1, tiled=True)

    experts = lax.axis_index("expert") * local + jnp.arange(local, dtype=jnp.int32)
    named = lax.all_gather(
        jnp.sum(
            jnp.where(
                routes[:, :, None] == jnp.arange(local * shards, dtype=jnp.int32), gates[:, :, None], 0.0
            ),
            axis=1,
        ),
        "expert",
        axis=0,
        tiled=True,
    )
    share = jnp.repeat(jnp.take(named, experts, axis=1), hidden_width, axis=1)
    tok, grad = to_columns(tokens), to_columns(out_grad)
    first = jnp.swapaxes(w_first, 0, 1).reshape(latent_width, local * hidden_width)
    second = w_second.reshape(local * hidden_width, latent_width)
    latent = total(dot(tok, w_in, ((1,), (0,))))
    grad_latent = total(dot(grad, w_out, ((1,), (0,))))
    active = jnp.maximum(dot(latent, first, ((1,), (0,))), 0.0)
    hidden = (share * active * active).astype(bf16)
    lat_out = total(dot(hidden, second, ((1,), (0,))))
    slope = (dot(grad_latent, second, ((1,), (1,))) * share * (2.0 * active)).astype(bf16)
    grad_in = total(dot(slope, first, ((1,), (1,))))
    grad_second = dot(hidden, grad_latent, ((0,), (0,))).astype(bf16)
    grad_first = dot(latent, slope, ((0,), (0,))).astype(bf16)
    return (
        to_rows(dot(lat_out, w_out, ((1,), (1,))).astype(bf16)),
        to_rows(dot(grad_in, w_in, ((1,), (1,))).astype(bf16)),
        dot(tok, grad_in, ((0,), (0,))),
        dot(grad, lat_out, ((0,), (0,))),
        jnp.swapaxes(grad_first.reshape(latent_width, local, hidden_width), 0, 1),
        grad_second.reshape(local, hidden_width, latent_width),
    )


def layer(*args):
    tokens, routes, w_first = args[0], args[1], args[5]
    count, experts = tokens.shape[0], w_first.shape[0] * lax.axis_size("expert")
    if 5 * count * routes.shape[1] // (2 * experts) >= count:
        return dense_body(*args)
    return body(*args)


def solution(mesh):
    placed = (
        P(("groups", "expert"), "dp"),
        P(("groups", "expert"), None),
        P(("groups", "expert"), None),
        P(("dp", "expert"), None),
        P(("dp", "expert"), None),
        P("expert", None, "dp"),
        P("expert", "dp", None),
        P(("groups", "expert"), "dp"),
    )
    return jax.shard_map(
        layer,
        mesh=mesh,
        in_specs=placed,
        out_specs=(
            P(("groups", "expert"), "dp"),
            P(("groups", "expert"), "dp"),
            P(("groups", "dp", "expert"), None),
            P(("groups", "dp", "expert"), None),
            P(("groups", "expert"), None, "dp"),
            P(("groups", "expert"), "dp", None),
        ),
        check_vma=False,
    )
```

```python
import functools

import jax
import jax.numpy as jnp
from jax import lax
from jax.experimental import pallas as pl
from jax.experimental.pallas import tpu as pltpu
from jax.sharding import PartitionSpec as P


def body(tokens, routes, gates, w_in, w_out, w_first, w_second, out_grad):
    in_full, out_full = (
        lax.all_gather(w_in, "expert", axis=0, tiled=True),
        lax.all_gather(w_out, "expert", axis=0, tiled=True),
    )
    token_count = tokens.shape[0]
    top_count = routes.shape[1]
    expert_local = w_first.shape[0]
    expert_shards = lax.axis_size("expert")
    expert_total = expert_local * expert_shards
    latent_width = w_in.shape[1]
    capacity = min(token_count, max(2, 5 * token_count * top_count // (2 * expert_total)))
    flat = routes.reshape(-1)
    onehot = (flat[:, None] == jnp.arange(expert_total, dtype=jnp.int32)[None, :]).astype(jnp.int32)
    slot = jnp.sum(onehot * (jnp.cumsum(onehot, axis=0) - 1), axis=1)
    dest = flat * capacity + slot
    weights = gates.reshape(-1, 1)

    def dp_total(value):
        return lax.psum(value.astype(jnp.bfloat16), "dp").astype(jnp.float32)

    def pack(route_rows):
        buffer = (
            jnp.zeros((expert_total * capacity, route_rows.shape[1]), route_rows.dtype)
            .at[dest]
            .set(route_rows)
        )
        return buffer.reshape(expert_shards, expert_local, capacity, route_rows.shape[1])

    def send(route_rows):
        share = latent_width // lax.axis_size("dp")
        columns = lax.dynamic_slice_in_dim(route_rows, lax.axis_index("dp") * share, share, 1)
        moved = lax.all_to_all(pack(columns), "expert", split_axis=0, concat_axis=0, tiled=True)
        return lax.all_gather(moved, "dp", axis=3, tiled=True)

    def combine_rows(buffer, scale):
        returned = lax.all_to_all(buffer, "expert", split_axis=0, concat_axis=0, tiled=True)
        rows = returned.reshape(expert_total * capacity, latent_width)[dest].astype(jnp.float32)
        if scale is not None:
            rows = scale * rows
        summed = jnp.sum(rows.reshape(token_count, top_count, latent_width), axis=1)
        return dp_total(summed).astype(jnp.bfloat16)

    latent = dp_total(jnp.dot(tokens, in_full, preferred_element_type=jnp.float32)).astype(
        jnp.bfloat16
    )
    arrived = send(jnp.repeat(latent, top_count, axis=0))
    before = jnp.einsum("sjcl,jlh->sjch", arrived, w_first, preferred_element_type=jnp.float32)
    hidden = jnp.square(jax.nn.relu(before)).astype(jnp.bfloat16)
    partial_out = jnp.einsum(
        "sjch,jhl->sjcl", hidden, w_second, preferred_element_type=jnp.float32
    ).astype(jnp.bfloat16)
    lat_out = combine_rows(partial_out, weights)
    mixed = jnp.dot(lat_out, out_full.T, preferred_element_type=jnp.float32).astype(jnp.bfloat16)
    grad_latent = dp_total(jnp.dot(out_grad, out_full, preferred_element_type=jnp.float32)).astype(
        jnp.bfloat16
    )
    route_grad = (weights * jnp.repeat(grad_latent, top_count, axis=0).astype(jnp.float32)).astype(
        jnp.bfloat16
    )
    incoming = send(route_grad)
    hidden_grad = jnp.einsum(
        "sjcl,jhl->sjch", incoming, w_second, preferred_element_type=jnp.float32
    )
    before_grad = (hidden_grad * 2.0 * jax.nn.relu(before)).astype(jnp.bfloat16)
    grad_second = jnp.einsum(
        "sjch,sjcl->jhl", hidden, incoming, preferred_element_type=jnp.float32
    ).astype(jnp.bfloat16)
    grad_first = jnp.einsum(
        "sjcl,sjch->jlh", arrived, before_grad, preferred_element_type=jnp.float32
    ).astype(jnp.bfloat16)
    back_piece = jnp.einsum(
        "sjch,jlh->sjcl", before_grad, w_first, preferred_element_type=jnp.float32
    ).astype(jnp.bfloat16)
    grad_in = combine_rows(back_piece, None)
    grad_tokens = jnp.dot(grad_in, in_full.T, preferred_element_type=jnp.float32).astype(
        jnp.bfloat16
    )
    first_term = jnp.dot(tokens.T, grad_in, preferred_element_type=jnp.float32)
    second_term = jnp.dot(out_grad.T, lat_out, preferred_element_type=jnp.float32)
    sums = lax.psum_scatter(
        jnp.concatenate([first_term, second_term], axis=1).astype(jnp.bfloat16),
        "expert",
        scatter_dimension=0,
        tiled=True,
    ).astype(jnp.float32)
    return (
        mixed,
        grad_tokens,
        sums[:, :latent_width],
        sums[:, latent_width:],
        grad_first,
        grad_second,
    )


CHUNKS = 2


def fused_kernel(
    shards,
    named_ref, tokens_ref, grad_ref, w_in_hbm, w_out_hbm, w_first_hbm, w_second_hbm,
    mixed_out, grad_tokens_out, grad_w_in_out, grad_w_out_out, grad_first_out, grad_second_out,
    w_in, w_out, first, second, cols, gates_all, share, twice, hidden, slope,
    part, from_core, half, from_x, quarter, from_z, whole, back,
    g_w_in, g_w_out, g_first, g_second,
    send_sems, recv_sems, local_sems,
):
    bf16, f32 = jnp.bfloat16, jnp.float32
    local, _, width = first.shape
    rows = from_x.shape[1]
    block = rows // shards
    depth = w_in.shape[0]
    wide, narrow = half.shape[2] * 2, half.shape[2]
    z, dp = lax.axis_index("expert"), lax.axis_index("dp")
    core, x = lax.rem(dp, 2), lax.div(dp, 2)
    core_mate = {"dp": x * 2 + 1 - core}
    x_mate = {"dp": (1 - x) * 2 + core}
    peers = [lax.rem(z + d, shards) for d in range(1, shards)]
    remote, near = [], []

    def at(index, size):
        return pl.ds(pl.multiple_of(index * size, size), size)

    def ship(src, dst, device):
        copy = pltpu.make_async_remote_copy(
            src_ref=src,
            dst_ref=dst,
            send_sem=send_sems.at[len(remote)],
            recv_sem=recv_sems.at[len(remote)],
            device_id=device,
            device_id_type=pl.DeviceIdType.MESH,
        )
        copy.start()
        remote.append(copy)
        return copy

    def move(src, dst):
        copy = pltpu.make_async_copy(src, dst, local_sems.at[len(near)])
        copy.start()
        near.append(copy)
        return copy

    def dot(a, b, dims):
        return lax.dot_general(a, b, (dims, ((), ())), preferred_element_type=f32)

    def arrive(copies):
        for copy in copies:
            copy.wait_recv()

    barrier = pltpu.get_barrier_semaphore()
    for device in [core_mate, x_mate] + [{"expert": q} for q in peers]:
        pl.semaphore_signal(
            barrier, inc=1, device_id=device, device_id_type=pl.DeviceIdType.MESH
        )
    loads = {}
    loads["w_in"] = move(w_in_hbm, w_in)
    loads["w_out"] = move(w_out_hbm, w_out)
    own = {}
    for h in range(CHUNKS):
        for a, source in enumerate((tokens_ref, grad_ref)):
            own[h, a] = move(
                source.at[pl.ds(h * block, block), at(z, depth)], cols.at[h, a, at(z, block), :]
            )
    own_gates = move(named_ref, gates_all.at[z])
    loads["first"] = move(w_first_hbm, first)
    loads["second"] = move(w_second_hbm, second)
    pl.semaphore_wait(barrier, shards + 1)

    incoming = {}
    for h in range(CHUNKS):
        for a, source in enumerate((tokens_ref, grad_ref)):
            incoming[h, a] = [
                ship(
                    source.at[pl.ds(h * block, block), at(q, depth)],
                    cols.at[h, a, at(z, block), :],
                    {"expert": q},
                )
                for q in peers
            ]
    gates_in = [ship(named_ref, gates_all.at[z], {"expert": q}) for q in peers]

    def gather_gates():
        own_gates.wait()
        arrive(gates_in)
        total = named_ref.shape[0]
        expert = lax.broadcasted_iota(jnp.int32, (total, local * width), 0)
        column = lax.broadcasted_iota(jnp.int32, (total, local * width), 1)
        pick = jnp.zeros((total, local * width), f32)
        for j in range(local):
            hit = (expert == z * local + j) & (column >= j * width) & (column < (j + 1) * width)
            pick = jnp.where(hit, 1.0, pick)
        for s in range(shards):
            value = lax.dot_general(
                gates_all[s], pick, (((0,), (0,)), ((), ())),
                precision=lax.Precision.HIGHEST, preferred_element_type=f32,
            )
            for h in range(CHUNKS):
                share[h, s * block : (s + 1) * block, :] = value[h * block : (h + 1) * block]

    def reduce(task, result, h, value):
        part[task] = value.astype(bf16)
        mine = core * 2 + x
        yours = core * 2 + 1 - x
        copy = ship(part.at[task, :, at(1 - core, narrow)], from_core.at[task], core_mate)
        yield
        arrive([copy])
        half[task, :, at(1 - x, narrow // 2)] = (
            part[task, :, at(yours, narrow // 2)].astype(f32)
            + from_core[task, :, at(1 - x, narrow // 2)].astype(f32)
        ).astype(bf16)
        copy = ship(half.at[task, :, at(1 - x, narrow // 2)], from_x.at[task], x_mate)
        yield
        arrive([copy])
        quarter[task] = (
            part[task, :, at(mine, narrow // 2)].astype(f32)
            + from_core[task, :, at(x, narrow // 2)].astype(f32)
            + from_x[task].astype(f32)
        ).astype(bf16)
        copies = [
            ship(quarter.at[task, at(q, block), :], from_z.at[task, d], {"expert": q})
            for d, q in enumerate(peers)
        ]
        yield
        arrive(copies)
        value = quarter[task, at(z, block), :].astype(f32)
        for d in range(shards - 1):
            value = value + from_z[task, d].astype(f32)
        spot = whole.at[result, pl.ds(pl.multiple_of(h * rows + z * block, block), block), at(mine, narrow // 2)]
        spot[...] = value.astype(bf16)
        copies = [ship(spot, spot, {"expert": q}) for q in peers]
        yield
        arrive(copies)
        spot = whole.at[result, pl.ds(h * rows, rows), at(mine, narrow // 2)]
        copy = ship(spot, spot, x_mate)
        yield
        arrive([copy])
        spot = whole.at[result, pl.ds(h * rows, rows), at(core, narrow)]
        copy = ship(spot, spot, core_mate)
        yield
        arrive([copy])

    def span(h):
        return slice(h * rows, (h + 1) * rows)

    def give_back(h, a, target):
        spots = target.at[pl.ds(h * block, block), at(z, depth)]
        move(back.at[h, a, at(z, block), :], spots)
        return [ship(back.at[h, a, at(q, block), :], spots, {"expert": q}) for q in peers]

    outgoing = []

    def forward(h):
        own[h, 0].wait()
        arrive(incoming[h, 0])
        if h == 0:
            loads["w_in"].wait()
        yield from reduce(h, 0, h, dot(cols[h, 0], w_in[...], ((1,), (0,))))
        if h == 0:
            loads["first"].wait()
            loads["second"].wait()
            gather_gates()
        for j in range(local):
            lanes = slice(j * width, (j + 1) * width)
            active = jnp.maximum(dot(whole[0, span(h), :], first[j], ((1,), (0,))), 0.0)
            scaled = share[h, :, lanes] * active
            hidden[span(h), lanes] = (scaled * active).astype(bf16)
            twice[h, :, lanes] = 2.0 * scaled
        yield from reduce(
            2 * CHUNKS + h, 2, h, dot(hidden[span(h), :], second[...], ((1,), (0,)))
        )
        back[h, 0] = dot(whole[2, span(h), :], w_out[...], ((1,), (1,))).astype(bf16)
        outgoing.extend(give_back(h, 0, mixed_out))

    def backward(h):
        own[h, 1].wait()
        arrive(incoming[h, 1])
        if h == 0:
            loads["w_out"].wait()
        yield from reduce(CHUNKS + h, 1, h, dot(cols[h, 1], w_out[...], ((1,), (0,))))
        slope[span(h), :] = (
            dot(whole[1, span(h), :], second[...], ((1,), (1,))) * twice[h]
        ).astype(bf16)
        value = dot(slope[span(h), 0:width], first[0], ((1,), (1,)))
        for j in range(1, local):
            lanes = slice(j * width, (j + 1) * width)
            value = value + dot(slope[span(h), lanes], first[j], ((1,), (1,)))
        yield from reduce(3 * CHUNKS + h, 3, h, value)
        back[h, 1] = dot(whole[3, span(h), :], w_in[...], ((1,), (1,))).astype(bf16)
        outgoing.extend(give_back(h, 1, grad_tokens_out))

    def weights():
        for _ in range(7):
            yield
        g_second[...] = dot(hidden[...], whole[1], ((0,), (0,))).astype(bf16)
        move(g_second, grad_second_out)
        yield
        for j in range(local):
            lanes = slice(j * width, (j + 1) * width)
            g_first[j] = dot(whole[0], slope[:, lanes], ((0,), (0,))).astype(bf16)
        move(g_first, grad_first_out)

    chains = []
    for h in range(CHUNKS):
        chains += [forward(h), backward(h)]
    chains.append(weights())
    while chains:
        for chain in list(chains):
            try:
                next(chain)
            except StopIteration:
                chains.remove(chain)

    def column(a):
        return jnp.concatenate([cols[h, a] for h in range(CHUNKS)], axis=0)

    g_w_out[...] = dot(column(1), whole[2], ((0,), (0,)))
    move(g_w_out, grad_w_out_out)
    g_w_in[...] = dot(column(0), whole[3], ((0,), (0,)))
    move(g_w_in, grad_w_in_out)
    arrive(outgoing)
    for copy in remote:
        copy.wait_send()
    for copy in near[2 * CHUNKS + 5 :]:
        copy.wait()


def fused_layer(tokens, routes, gates, w_in, w_out, w_first, w_second, out_grad):
    bf16, f32 = jnp.bfloat16, jnp.float32
    shards = lax.axis_size("expert")
    local, latent, width = w_first.shape
    count, depth = tokens.shape[0], w_in.shape[0]
    rows = count * shards // CHUNKS
    tasks, ships, moves = 4 * CHUNKS, 4 * CHUNKS * (2 * shards + 2), 8 * CHUNKS + 16
    ships += (4 * CHUNKS + 1) * (shards - 1)
    experts = jnp.arange(local * shards, dtype=jnp.int32)[:, None, None]
    named = jnp.sum(jnp.where(routes.T[None] == experts, gates.T[None], 0.0), axis=1)
    both = local * width
    shape = jax.ShapeDtypeStruct
    outs = pl.pallas_call(
        functools.partial(fused_kernel, shards),
        out_shape=[
            shape(tokens.shape, bf16),
            shape(tokens.shape, bf16),
            shape(w_in.shape, f32),
            shape(w_out.shape, f32),
            shape(w_first.shape, bf16),
            shape((both, latent), bf16),
        ],
        in_specs=[pl.BlockSpec(memory_space=pltpu.VMEM)] + [pl.BlockSpec(memory_space=pl.ANY)] * 6,
        out_specs=[pl.BlockSpec(memory_space=pl.ANY)] * 6,
        scratch_shapes=[
            pltpu.VMEM(w_in.shape, bf16),
            pltpu.VMEM(w_out.shape, bf16),
            pltpu.VMEM(w_first.shape, bf16),
            pltpu.VMEM((both, latent), bf16),
            pltpu.VMEM((CHUNKS, 2, rows, depth), bf16),
            pltpu.VMEM((shards,) + named.shape, f32),
            pltpu.VMEM((CHUNKS, rows, both), f32),
            pltpu.VMEM((CHUNKS, rows, both), f32),
            pltpu.VMEM((CHUNKS * rows, both), bf16),
            pltpu.VMEM((CHUNKS * rows, both), bf16),
            pltpu.VMEM((tasks, rows, latent), bf16),
            pltpu.VMEM((tasks, rows, latent // 2), bf16),
            pltpu.VMEM((tasks, rows, latent // 2), bf16),
            pltpu.VMEM((tasks, rows, latent // 4), bf16),
            pltpu.VMEM((tasks, rows, latent // 4), bf16),
            pltpu.VMEM((tasks, shards - 1, rows // shards, latent // 4), bf16),
            pltpu.VMEM((4, CHUNKS * rows, latent), bf16),
            pltpu.VMEM((CHUNKS, 2, rows, depth), bf16),
            pltpu.VMEM(w_in.shape, f32),
            pltpu.VMEM(w_out.shape, f32),
            pltpu.VMEM(w_first.shape, bf16),
            pltpu.VMEM((both, latent), bf16),
            pltpu.SemaphoreType.DMA((ships,)),
            pltpu.SemaphoreType.DMA((ships,)),
            pltpu.SemaphoreType.DMA((moves,)),
        ],
        compiler_params=pltpu.CompilerParams(
            collective_id=0, has_side_effects=True, vmem_limit_bytes=56 * 1024 * 1024
        ),
        name="fused_layer",
    )(named, tokens, out_grad, w_in, w_out, w_first, w_second.reshape(both, latent))
    return (*outs[:5], outs[5].reshape(w_second.shape))


def layer(*args):
    tokens, routes, w_first = args[0], args[1], args[5]
    count, experts = tokens.shape[0], w_first.shape[0] * lax.axis_size("expert")
    if 5 * count * routes.shape[1] // (2 * experts) >= count and lax.axis_size("dp") == 4:
        return fused_layer(*args)
    return body(*args)


def solution(mesh):
    placed = (
        P(("groups", "expert"), "dp"),
        P(("groups", "expert"), None),
        P(("groups", "expert"), None),
        P(("dp", "expert"), None),
        P(("dp", "expert"), None),
        P("expert", None, "dp"),
        P("expert", "dp", None),
        P(("groups", "expert"), "dp"),
    )
    return jax.shard_map(
        layer,
        mesh=mesh,
        in_specs=placed,
        out_specs=(
            P(("groups", "expert"), "dp"),
            P(("groups", "expert"), "dp"),
            P(("groups", "dp", "expert"), None),
            P(("groups", "dp", "expert"), None),
            P(("groups", "expert"), None, "dp"),
            P(("groups", "expert"), "dp", None),
        ),
        check_vma=False,
    )
```

```python
import functools

import jax
import jax.numpy as jnp
from jax import lax
from jax.experimental import pallas as pl
from jax.experimental.pallas import tpu as pltpu
from jax.sharding import PartitionSpec as P


def body(tokens, routes, gates, w_in, w_out, w_first, w_second, out_grad):
    in_full, out_full = (
        lax.all_gather(w_in, "expert", axis=0, tiled=True),
        lax.all_gather(w_out, "expert", axis=0, tiled=True),
    )
    token_count = tokens.shape[0]
    top_count = routes.shape[1]
    expert_local = w_first.shape[0]
    expert_shards = lax.axis_size("expert")
    expert_total = expert_local * expert_shards
    latent_width = w_in.shape[1]
    capacity = min(token_count, max(2, 5 * token_count * top_count // (2 * expert_total)))
    flat = routes.reshape(-1)
    onehot = (flat[:, None] == jnp.arange(expert_total, dtype=jnp.int32)[None, :]).astype(jnp.int32)
    slot = jnp.sum(onehot * (jnp.cumsum(onehot, axis=0) - 1), axis=1)
    dest = flat * capacity + slot
    weights = gates.reshape(-1, 1)

    def dp_total(value):
        return lax.psum(value.astype(jnp.bfloat16), "dp").astype(jnp.float32)

    def pack(route_rows):
        buffer = (
            jnp.zeros((expert_total * capacity, route_rows.shape[1]), route_rows.dtype)
            .at[dest]
            .set(route_rows)
        )
        return buffer.reshape(expert_shards, expert_local, capacity, route_rows.shape[1])

    def send(route_rows):
        share = latent_width // lax.axis_size("dp")
        columns = lax.dynamic_slice_in_dim(route_rows, lax.axis_index("dp") * share, share, 1)
        moved = lax.all_to_all(pack(columns), "expert", split_axis=0, concat_axis=0, tiled=True)
        return lax.all_gather(moved, "dp", axis=3, tiled=True)

    def combine_rows(buffer, scale):
        returned = lax.all_to_all(buffer, "expert", split_axis=0, concat_axis=0, tiled=True)
        rows = returned.reshape(expert_total * capacity, latent_width)[dest].astype(jnp.float32)
        if scale is not None:
            rows = scale * rows
        summed = jnp.sum(rows.reshape(token_count, top_count, latent_width), axis=1)
        return dp_total(summed).astype(jnp.bfloat16)

    latent = dp_total(jnp.dot(tokens, in_full, preferred_element_type=jnp.float32)).astype(
        jnp.bfloat16
    )
    arrived = send(jnp.repeat(latent, top_count, axis=0))
    before = jnp.einsum("sjcl,jlh->sjch", arrived, w_first, preferred_element_type=jnp.float32)
    hidden = jnp.square(jax.nn.relu(before)).astype(jnp.bfloat16)
    partial_out = jnp.einsum(
        "sjch,jhl->sjcl", hidden, w_second, preferred_element_type=jnp.float32
    ).astype(jnp.bfloat16)
    lat_out = combine_rows(partial_out, weights)
    mixed = jnp.dot(lat_out, out_full.T, preferred_element_type=jnp.float32).astype(jnp.bfloat16)
    grad_latent = dp_total(jnp.dot(out_grad, out_full, preferred_element_type=jnp.float32)).astype(
        jnp.bfloat16
    )
    route_grad = (weights * jnp.repeat(grad_latent, top_count, axis=0).astype(jnp.float32)).astype(
        jnp.bfloat16
    )
    incoming = send(route_grad)
    hidden_grad = jnp.einsum(
        "sjcl,jhl->sjch", incoming, w_second, preferred_element_type=jnp.float32
    )
    before_grad = (hidden_grad * 2.0 * jax.nn.relu(before)).astype(jnp.bfloat16)
    grad_second = jnp.einsum(
        "sjch,sjcl->jhl", hidden, incoming, preferred_element_type=jnp.float32
    ).astype(jnp.bfloat16)
    grad_first = jnp.einsum(
        "sjcl,sjch->jlh", arrived, before_grad, preferred_element_type=jnp.float32
    ).astype(jnp.bfloat16)
    back_piece = jnp.einsum(
        "sjch,jlh->sjcl", before_grad, w_first, preferred_element_type=jnp.float32
    ).astype(jnp.bfloat16)
    grad_in = combine_rows(back_piece, None)
    grad_tokens = jnp.dot(grad_in, in_full.T, preferred_element_type=jnp.float32).astype(
        jnp.bfloat16
    )
    first_term = jnp.dot(tokens.T, grad_in, preferred_element_type=jnp.float32)
    second_term = jnp.dot(out_grad.T, lat_out, preferred_element_type=jnp.float32)
    sums = lax.psum_scatter(
        jnp.concatenate([first_term, second_term], axis=1).astype(jnp.bfloat16),
        "expert",
        scatter_dimension=0,
        tiled=True,
    ).astype(jnp.float32)
    return (
        mixed,
        grad_tokens,
        sums[:, :latent_width],
        sums[:, latent_width:],
        grad_first,
        grad_second,
    )


CHUNKS = 2
STAGGER = 1


def fused_kernel(
    shards,
    named_ref, tokens_ref, grad_ref, w_in_hbm, w_out_hbm, w_first_hbm, w_second_hbm,
    mixed_out, grad_tokens_out, grad_w_in_out, grad_w_out_out, grad_first_out, grad_second_out,
    w_in, w_out, first, second, cols, gates_all, share, twice, hidden, slope,
    part, from_core, half, from_x, quarter, from_z, whole, back,
    g_w_in, g_w_out, g_first, g_second,
    send_sems, recv_sems, local_sems,
):
    bf16, f32 = jnp.bfloat16, jnp.float32
    local, _, width = first.shape
    rows = from_x.shape[1]
    block = rows // shards
    depth = w_in.shape[0]
    wide, narrow = half.shape[2] * 2, half.shape[2]
    z, dp = lax.axis_index("expert"), lax.axis_index("dp")
    core, x = lax.rem(dp, 2), lax.div(dp, 2)
    core_mate = {"dp": x * 2 + 1 - core}
    x_mate = {"dp": (1 - x) * 2 + core}
    peers = [lax.rem(z + d, shards) for d in range(1, shards)]
    remote, near = [], []

    def at(index, size):
        return pl.ds(pl.multiple_of(index * size, size), size)

    def ship(src, dst, device):
        copy = pltpu.make_async_remote_copy(
            src_ref=src,
            dst_ref=dst,
            send_sem=send_sems.at[len(remote)],
            recv_sem=recv_sems.at[len(remote)],
            device_id=device,
            device_id_type=pl.DeviceIdType.MESH,
        )
        copy.start()
        remote.append(copy)
        return copy

    def move(src, dst):
        copy = pltpu.make_async_copy(src, dst, local_sems.at[len(near)])
        copy.start()
        near.append(copy)
        return copy

    def dot(a, b, dims):
        return lax.dot_general(a, b, (dims, ((), ())), preferred_element_type=f32)

    def arrive(copies):
        for copy in copies:
            copy.wait_recv()

    barrier = pltpu.get_barrier_semaphore()
    for device in [core_mate, x_mate] + [{"expert": q} for q in peers]:
        pl.semaphore_signal(
            barrier, inc=1, device_id=device, device_id_type=pl.DeviceIdType.MESH
        )
    loads = {}
    loads["w_in"] = move(w_in_hbm, w_in)
    loads["w_out"] = move(w_out_hbm, w_out)
    own = {}
    for h in range(CHUNKS):
        for a, source in enumerate((tokens_ref, grad_ref)):
            own[h, a] = move(
                source.at[pl.ds(h * block, block), at(z, depth)], cols.at[h, a, at(z, block), :]
            )
    own_gates = move(named_ref, gates_all.at[z])
    loads["first"] = move(w_first_hbm, first)
    loads["second"] = move(w_second_hbm, second)
    pl.semaphore_wait(barrier, shards + 1)

    incoming = {}
    for h in range(CHUNKS):
        for a, source in enumerate((tokens_ref, grad_ref)):
            incoming[h, a] = [
                ship(
                    source.at[pl.ds(h * block, block), at(q, depth)],
                    cols.at[h, a, at(z, block), :],
                    {"expert": q},
                )
                for q in peers
            ]
    gates_in = [ship(named_ref, gates_all.at[z], {"expert": q}) for q in peers]

    def gather_gates():
        own_gates.wait()
        arrive(gates_in)
        total = named_ref.shape[0]
        expert = lax.broadcasted_iota(jnp.int32, (total, local * width), 0)
        column = lax.broadcasted_iota(jnp.int32, (total, local * width), 1)
        pick = jnp.zeros((total, local * width), f32)
        for j in range(local):
            hit = (expert == z * local + j) & (column >= j * width) & (column < (j + 1) * width)
            pick = jnp.where(hit, 1.0, pick)
        for s in range(shards):
            value = lax.dot_general(
                gates_all[s], pick, (((0,), (0,)), ((), ())),
                precision=lax.Precision.HIGHEST, preferred_element_type=f32,
            )
            for h in range(CHUNKS):
                share[h, s * block : (s + 1) * block, :] = value[h * block : (h + 1) * block]

    def reduce(task, result, h, value):
        part[task] = value.astype(bf16)
        mine = core * 2 + x
        yours = core * 2 + 1 - x
        copy = ship(part.at[task, :, at(1 - core, narrow)], from_core.at[task], core_mate)
        yield
        arrive([copy])
        half[task, :, at(1 - x, narrow // 2)] = (
            part[task, :, at(yours, narrow // 2)].astype(f32)
            + from_core[task, :, at(1 - x, narrow // 2)].astype(f32)
        ).astype(bf16)
        copy = ship(half.at[task, :, at(1 - x, narrow // 2)], from_x.at[task], x_mate)
        yield
        arrive([copy])
        quarter[task] = (
            part[task, :, at(mine, narrow // 2)].astype(f32)
            + from_core[task, :, at(x, narrow // 2)].astype(f32)
            + from_x[task].astype(f32)
        ).astype(bf16)
        copies = [
            ship(quarter.at[task, at(q, block), :], from_z.at[task, d], {"expert": q})
            for d, q in enumerate(peers)
        ]
        yield
        arrive(copies)
        value = quarter[task, at(z, block), :].astype(f32)
        for d in range(shards - 1):
            value = value + from_z[task, d].astype(f32)
        spot = whole.at[result, pl.ds(pl.multiple_of(h * rows + z * block, block), block), at(mine, narrow // 2)]
        spot[...] = value.astype(bf16)
        copies = [ship(spot, spot, {"expert": q}) for q in peers]
        yield
        arrive(copies)
        spot = whole.at[result, pl.ds(h * rows, rows), at(mine, narrow // 2)]
        copy = ship(spot, spot, x_mate)
        yield
        arrive([copy])
        spot = whole.at[result, pl.ds(h * rows, rows), at(core, narrow)]
        copy = ship(spot, spot, core_mate)
        yield
        arrive([copy])

    def span(h):
        return slice(h * rows, (h + 1) * rows)

    def give_back(h, a, target):
        spots = target.at[pl.ds(h * block, block), at(z, depth)]
        move(back.at[h, a, at(z, block), :], spots)
        return [ship(back.at[h, a, at(q, block), :], spots, {"expert": q}) for q in peers]

    outgoing = []

    def forward(h):
        own[h, 0].wait()
        arrive(incoming[h, 0])
        if h == 0:
            loads["w_in"].wait()
        yield from reduce(h, 0, h, dot(cols[h, 0], w_in[...], ((1,), (0,))))
        if h == 0:
            loads["first"].wait()
            loads["second"].wait()
            gather_gates()
        for j in range(local):
            lanes = slice(j * width, (j + 1) * width)
            active = jnp.maximum(dot(whole[0, span(h), :], first[j], ((1,), (0,))), 0.0)
            scaled = share[h, :, lanes] * active
            hidden[span(h), lanes] = (scaled * active).astype(bf16)
            twice[h, :, lanes] = 2.0 * scaled
        yield from reduce(
            2 * CHUNKS + h, 2, h, dot(hidden[span(h), :], second[...], ((1,), (0,)))
        )
        back[h, 0] = dot(whole[2, span(h), :], w_out[...], ((1,), (1,))).astype(bf16)
        outgoing.extend(give_back(h, 0, mixed_out))

    def backward(h):
        own[h, 1].wait()
        arrive(incoming[h, 1])
        if h == 0:
            loads["w_out"].wait()
        yield from reduce(CHUNKS + h, 1, h, dot(cols[h, 1], w_out[...], ((1,), (0,))))
        slope[span(h), :] = (
            dot(whole[1, span(h), :], second[...], ((1,), (1,))) * twice[h]
        ).astype(bf16)
        value = dot(slope[span(h), 0:width], first[0], ((1,), (1,)))
        for j in range(1, local):
            lanes = slice(j * width, (j + 1) * width)
            value = value + dot(slope[span(h), lanes], first[j], ((1,), (1,)))
        yield from reduce(3 * CHUNKS + h, 3, h, value)
        back[h, 1] = dot(whole[3, span(h), :], w_in[...], ((1,), (1,))).astype(bf16)
        outgoing.extend(give_back(h, 1, grad_tokens_out))

    def weights():
        g_second[...] = dot(hidden[...], whole[1], ((0,), (0,))).astype(bf16)
        move(g_second, grad_second_out)
        yield
        for j in range(local):
            lanes = slice(j * width, (j + 1) * width)
            g_first[j] = dot(whole[0], slope[:, lanes], ((0,), (0,))).astype(bf16)
        move(g_first, grad_first_out)

    chains = []
    for h in range(CHUNKS):
        chains += [(STAGGER * len(chains), forward(h))]
        chains += [(STAGGER * len(chains), backward(h))]
    chains.append((chains[-1][0] + 7, weights()))
    turn = 0
    while chains:
        for start, chain in list(chains):
            if turn >= start:
                try:
                    next(chain)
                except StopIteration:
                    chains.remove((start, chain))
        turn += 1

    def column(a):
        return jnp.concatenate([cols[h, a] for h in range(CHUNKS)], axis=0)

    g_w_out[...] = dot(column(1), whole[2], ((0,), (0,)))
    move(g_w_out, grad_w_out_out)
    g_w_in[...] = dot(column(0), whole[3], ((0,), (0,)))
    move(g_w_in, grad_w_in_out)
    arrive(outgoing)
    for copy in remote:
        copy.wait_send()
    for copy in near[2 * CHUNKS + 5 :]:
        copy.wait()


def settle_kernel(count, *refs):
    sources, targets, held, sems = refs[:count], refs[count : 2 * count], refs[2 * count : -1], refs[-1]
    loads = [
        pltpu.make_async_copy(sources[i], held[i], sems.at[0, i]) for i in range(count)
    ]
    stores = [
        pltpu.make_async_copy(held[i], targets[i], sems.at[1, i]) for i in range(count)
    ]
    for copy in loads:
        copy.start()
    for load, store in zip(loads, stores):
        load.wait()
        store.start()
    for copy in stores:
        copy.wait()


def settle(*arrays):
    count = len(arrays)
    return pl.pallas_call(
        functools.partial(settle_kernel, count),
        out_shape=[jax.ShapeDtypeStruct(a.shape, a.dtype) for a in arrays],
        in_specs=[pl.BlockSpec(memory_space=pl.ANY)] * count,
        out_specs=[pl.BlockSpec(memory_space=pl.ANY)] * count,
        scratch_shapes=[pltpu.VMEM(a.shape, a.dtype) for a in arrays]
        + [pltpu.SemaphoreType.DMA((2, count))],
        compiler_params=pltpu.CompilerParams(vmem_limit_bytes=56 * 1024 * 1024),
        name="settle",
    )(*arrays)


def fused_layer(tokens, routes, gates, w_in, w_out, w_first, w_second, out_grad):
    bf16, f32 = jnp.bfloat16, jnp.float32
    shards = lax.axis_size("expert")
    local, latent, width = w_first.shape
    count, depth = tokens.shape[0], w_in.shape[0]
    rows = count * shards // CHUNKS
    tasks, ships, moves = 4 * CHUNKS, 4 * CHUNKS * (2 * shards + 2), 8 * CHUNKS + 16
    ships += (4 * CHUNKS + 1) * (shards - 1)
    experts = jnp.arange(local * shards, dtype=jnp.int32)[:, None, None]
    named = jnp.sum(jnp.where(routes.T[None] == experts, gates.T[None], 0.0), axis=1)
    both = local * width
    shape = jax.ShapeDtypeStruct
    outs = pl.pallas_call(
        functools.partial(fused_kernel, shards),
        out_shape=[
            shape(tokens.shape, bf16),
            shape(tokens.shape, bf16),
            shape(w_in.shape, f32),
            shape(w_out.shape, f32),
            shape(w_first.shape, bf16),
            shape((both, latent), bf16),
        ],
        in_specs=[pl.BlockSpec(memory_space=pltpu.VMEM)] + [pl.BlockSpec(memory_space=pl.ANY)] * 6,
        out_specs=[pl.BlockSpec(memory_space=pl.ANY)] * 6,
        scratch_shapes=[
            pltpu.VMEM(w_in.shape, bf16),
            pltpu.VMEM(w_out.shape, bf16),
            pltpu.VMEM(w_first.shape, bf16),
            pltpu.VMEM((both, latent), bf16),
            pltpu.VMEM((CHUNKS, 2, rows, depth), bf16),
            pltpu.VMEM((shards,) + named.shape, f32),
            pltpu.VMEM((CHUNKS, rows, both), f32),
            pltpu.VMEM((CHUNKS, rows, both), f32),
            pltpu.VMEM((CHUNKS * rows, both), bf16),
            pltpu.VMEM((CHUNKS * rows, both), bf16),
            pltpu.VMEM((tasks, rows, latent), bf16),
            pltpu.VMEM((tasks, rows, latent // 2), bf16),
            pltpu.VMEM((tasks, rows, latent // 2), bf16),
            pltpu.VMEM((tasks, rows, latent // 4), bf16),
            pltpu.VMEM((tasks, rows, latent // 4), bf16),
            pltpu.VMEM((tasks, shards - 1, rows // shards, latent // 4), bf16),
            pltpu.VMEM((4, CHUNKS * rows, latent), bf16),
            pltpu.VMEM((CHUNKS, 2, rows, depth), bf16),
            pltpu.VMEM(w_in.shape, f32),
            pltpu.VMEM(w_out.shape, f32),
            pltpu.VMEM(w_first.shape, bf16),
            pltpu.VMEM((both, latent), bf16),
            pltpu.SemaphoreType.DMA((ships,)),
            pltpu.SemaphoreType.DMA((ships,)),
            pltpu.SemaphoreType.DMA((moves,)),
        ],
        compiler_params=pltpu.CompilerParams(
            collective_id=0, has_side_effects=True, vmem_limit_bytes=56 * 1024 * 1024
        ),
        name="fused_layer",
    )(named, tokens, out_grad, w_in, w_out, w_first, w_second.reshape(both, latent))
    outs = settle(*outs)
    return (*outs[:5], outs[5].reshape(w_second.shape))


def layer(*args):
    tokens, routes, w_first = args[0], args[1], args[5]
    count, experts = tokens.shape[0], w_first.shape[0] * lax.axis_size("expert")
    if 5 * count * routes.shape[1] // (2 * experts) >= count and lax.axis_size("dp") == 4:
        return fused_layer(*args)
    return body(*args)


def solution(mesh):
    placed = (
        P(("groups", "expert"), "dp"),
        P(("groups", "expert"), None),
        P(("groups", "expert"), None),
        P(("dp", "expert"), None),
        P(("dp", "expert"), None),
        P("expert", None, "dp"),
        P("expert", "dp", None),
        P(("groups", "expert"), "dp"),
    )
    return jax.shard_map(
        layer,
        mesh=mesh,
        in_specs=placed,
        out_specs=(
            P(("groups", "expert"), "dp"),
            P(("groups", "expert"), "dp"),
            P(("groups", "dp", "expert"), None),
            P(("groups", "dp", "expert"), None),
            P(("groups", "expert"), None, "dp"),
            P(("groups", "expert"), "dp", None),
        ),
        check_vma=False,
    )
```

```python
import functools

import jax
import jax.numpy as jnp
from jax import lax
from jax.experimental import pallas as pl
from jax.experimental.pallas import tpu as pltpu
from jax.sharding import PartitionSpec as P


def body(tokens, routes, gates, w_in, w_out, w_first, w_second, out_grad):
    in_full, out_full = (
        lax.all_gather(w_in, "expert", axis=0, tiled=True),
        lax.all_gather(w_out, "expert", axis=0, tiled=True),
    )
    token_count = tokens.shape[0]
    top_count = routes.shape[1]
    expert_local = w_first.shape[0]
    expert_shards = lax.axis_size("expert")
    expert_total = expert_local * expert_shards
    latent_width = w_in.shape[1]
    capacity = min(token_count, max(2, 5 * token_count * top_count // (2 * expert_total)))
    flat = routes.reshape(-1)
    onehot = (flat[:, None] == jnp.arange(expert_total, dtype=jnp.int32)[None, :]).astype(jnp.int32)
    slot = jnp.sum(onehot * (jnp.cumsum(onehot, axis=0) - 1), axis=1)
    dest = flat * capacity + slot
    weights = gates.reshape(-1, 1)

    def dp_total(value):
        return lax.psum(value.astype(jnp.bfloat16), "dp").astype(jnp.float32)

    def pack(route_rows):
        buffer = (
            jnp.zeros((expert_total * capacity, route_rows.shape[1]), route_rows.dtype)
            .at[dest]
            .set(route_rows)
        )
        return buffer.reshape(expert_shards, expert_local, capacity, route_rows.shape[1])

    def send(route_rows):
        share = latent_width // lax.axis_size("dp")
        columns = lax.dynamic_slice_in_dim(route_rows, lax.axis_index("dp") * share, share, 1)
        moved = lax.all_to_all(pack(columns), "expert", split_axis=0, concat_axis=0, tiled=True)
        return lax.all_gather(moved, "dp", axis=3, tiled=True)

    def combine_rows(buffer, scale):
        returned = lax.all_to_all(buffer, "expert", split_axis=0, concat_axis=0, tiled=True)
        rows = returned.reshape(expert_total * capacity, latent_width)[dest].astype(jnp.float32)
        if scale is not None:
            rows = scale * rows
        summed = jnp.sum(rows.reshape(token_count, top_count, latent_width), axis=1)
        return dp_total(summed).astype(jnp.bfloat16)

    latent = dp_total(jnp.dot(tokens, in_full, preferred_element_type=jnp.float32)).astype(
        jnp.bfloat16
    )
    arrived = send(jnp.repeat(latent, top_count, axis=0))
    before = jnp.einsum("sjcl,jlh->sjch", arrived, w_first, preferred_element_type=jnp.float32)
    hidden = jnp.square(jax.nn.relu(before)).astype(jnp.bfloat16)
    partial_out = jnp.einsum(
        "sjch,jhl->sjcl", hidden, w_second, preferred_element_type=jnp.float32
    ).astype(jnp.bfloat16)
    lat_out = combine_rows(partial_out, weights)
    mixed = jnp.dot(lat_out, out_full.T, preferred_element_type=jnp.float32).astype(jnp.bfloat16)
    grad_latent = dp_total(jnp.dot(out_grad, out_full, preferred_element_type=jnp.float32)).astype(
        jnp.bfloat16
    )
    route_grad = (weights * jnp.repeat(grad_latent, top_count, axis=0).astype(jnp.float32)).astype(
        jnp.bfloat16
    )
    incoming = send(route_grad)
    hidden_grad = jnp.einsum(
        "sjcl,jhl->sjch", incoming, w_second, preferred_element_type=jnp.float32
    )
    before_grad = (hidden_grad * 2.0 * jax.nn.relu(before)).astype(jnp.bfloat16)
    grad_second = jnp.einsum(
        "sjch,sjcl->jhl", hidden, incoming, preferred_element_type=jnp.float32
    ).astype(jnp.bfloat16)
    grad_first = jnp.einsum(
        "sjcl,sjch->jlh", arrived, before_grad, preferred_element_type=jnp.float32
    ).astype(jnp.bfloat16)
    back_piece = jnp.einsum(
        "sjch,jlh->sjcl", before_grad, w_first, preferred_element_type=jnp.float32
    ).astype(jnp.bfloat16)
    grad_in = combine_rows(back_piece, None)
    grad_tokens = jnp.dot(grad_in, in_full.T, preferred_element_type=jnp.float32).astype(
        jnp.bfloat16
    )
    first_term = jnp.dot(tokens.T, grad_in, preferred_element_type=jnp.float32)
    second_term = jnp.dot(out_grad.T, lat_out, preferred_element_type=jnp.float32)
    sums = lax.psum_scatter(
        jnp.concatenate([first_term, second_term], axis=1).astype(jnp.bfloat16),
        "expert",
        scatter_dimension=0,
        tiled=True,
    ).astype(jnp.float32)
    return (
        mixed,
        grad_tokens,
        sums[:, :latent_width],
        sums[:, latent_width:],
        grad_first,
        grad_second,
    )


CHUNKS = 2
STAGGER = 1


def fused_kernel(
    shards,
    named_ref, tokens_ref, grad_ref, w_in_hbm, w_out_hbm, w_first_hbm, w_second_hbm,
    mixed_out, grad_tokens_out, grad_w_in_out, grad_w_out_out, grad_first_out, grad_second_out,
    w_in, w_out, first, second, cols, gates_all, share, twice, hidden, slope,
    part, from_core, half, from_x, quarter, from_near, pair, from_far, whole, back,
    g_w_in, g_w_out, g_first, g_second,
    send_sems, recv_sems, local_sems,
):
    bf16, f32 = jnp.bfloat16, jnp.float32
    local, _, width = first.shape
    block = from_far.shape[1]
    rows = block * shards
    depth = w_in.shape[0]
    wide, narrow = part.shape[4], from_core.shape[4]
    z, dp = lax.axis_index("expert"), lax.axis_index("dp")
    core, x = lax.rem(dp, 2), lax.div(dp, 2)
    core_mate = {"dp": x * 2 + 1 - core}
    x_mate = {"dp": (1 - x) * 2 + core}
    peers = [lax.rem(z + d, shards) for d in range(1, shards)]
    low, high = lax.rem(z, 2), lax.div(z, 2)
    near_mate, far_mate = {"expert": 2 * high + 1 - low}, {"expert": 2 * (1 - high) + low}
    remote, near = [], []

    def at(index, size):
        return pl.ds(pl.multiple_of(index * size, size), size)

    def ship(src, dst, device):
        copy = pltpu.make_async_remote_copy(
            src_ref=src,
            dst_ref=dst,
            send_sem=send_sems.at[len(remote)],
            recv_sem=recv_sems.at[len(remote)],
            device_id=device,
            device_id_type=pl.DeviceIdType.MESH,
        )
        copy.start()
        remote.append(copy)
        return copy

    def move(src, dst):
        copy = pltpu.make_async_copy(src, dst, local_sems.at[len(near)])
        copy.start()
        near.append(copy)
        return copy

    def dot(a, b, dims):
        return lax.dot_general(a, b, (dims, ((), ())), preferred_element_type=f32)

    def arrive(copies):
        for copy in copies:
            copy.wait_recv()

    barrier = pltpu.get_barrier_semaphore()
    for device in [core_mate, x_mate] + [{"expert": q} for q in peers]:
        pl.semaphore_signal(
            barrier, inc=1, device_id=device, device_id_type=pl.DeviceIdType.MESH
        )
    loads = {}
    loads["w_in"] = move(w_in_hbm, w_in)
    loads["w_out"] = move(w_out_hbm, w_out)
    own = {}
    for h in range(CHUNKS):
        for a, source in enumerate((tokens_ref, grad_ref)):
            own[h, a] = move(
                source.at[pl.ds(h * block, block), at(z, depth)], cols.at[h, a, at(z, block), :]
            )
    own_gates = move(named_ref, gates_all.at[z])
    loads["first"] = move(w_first_hbm, first)
    loads["second"] = move(w_second_hbm, second)
    pl.semaphore_wait(barrier, shards + 1)

    incoming = {}
    for h in range(CHUNKS):
        for a, source in enumerate((tokens_ref, grad_ref)):
            incoming[h, a] = [
                ship(
                    source.at[pl.ds(h * block, block), at(q, depth)],
                    cols.at[h, a, at(z, block), :],
                    {"expert": q},
                )
                for q in peers
            ]
    gates_in = [ship(named_ref, gates_all.at[z], {"expert": q}) for q in peers]

    def gather_gates():
        own_gates.wait()
        arrive(gates_in)
        total = named_ref.shape[0]
        expert = lax.broadcasted_iota(jnp.int32, (total, local * width), 0)
        column = lax.broadcasted_iota(jnp.int32, (total, local * width), 1)
        pick = jnp.zeros((total, local * width), f32)
        for j in range(local):
            hit = (expert == z * local + j) & (column >= j * width) & (column < (j + 1) * width)
            pick = jnp.where(hit, 1.0, pick)
        for s in range(shards):
            value = lax.dot_general(
                gates_all[s], pick, (((0,), (0,)), ((), ())),
                precision=lax.Precision.HIGHEST, preferred_element_type=f32,
            )
            for h in range(CHUNKS):
                share[h, s * block : (s + 1) * block, :] = value[h * block : (h + 1) * block]

    def reduce(task, result, h, value):
        mine, yours = core * 2 + x, core * 2 + 1 - x
        fine = narrow // 2

        def rows_of(index):
            start = pl.multiple_of(h * rows + index * block, block)
            return whole.at[result, pl.ds(start, block), at(mine, fine)]

        def spread(index):
            spot = rows_of(index)
            x_copies.append(ship(spot, spot, x_mate))
            core_copies.append(ship(spot, spot, core_mate))

        x_copies, core_copies = [], []
        part[task] = value.astype(bf16).reshape(2, 2, block, wide)
        copy = ship(part.at[task, :, :, :, at(1 - core, narrow)], from_core.at[task], core_mate)
        yield
        arrive([copy])
        half[task] = (
            part[task, :, :, :, at(yours, fine)].astype(f32)
            + from_core[task, :, :, :, at(1 - x, fine)].astype(f32)
        ).astype(bf16)
        first_copy, second_copy = [
            ship(half.at[task, :, side], from_x.at[task, :, side], x_mate)
            for side in (1 - low, low)
        ]
        yield
        arrive([first_copy])
        quarter[task] = (
            part[task, :, 1 - low, :, at(mine, fine)].astype(f32)
            + from_core[task, :, 1 - low, :, at(x, fine)].astype(f32)
            + from_x[task, :, 1 - low].astype(f32)
        ).astype(bf16)
        copy = ship(quarter.at[task], from_near.at[task], near_mate)
        yield
        arrive([second_copy, copy])

        def summed(side):
            return (
                part[task, side, low, :, at(mine, fine)].astype(f32)
                + from_core[task, side, low, :, at(x, fine)].astype(f32)
                + from_x[task, side, low].astype(f32)
                + from_near[task, side].astype(f32)
            )

        pair[task] = summed(1 - high).astype(bf16)
        copy = ship(pair.at[task], from_far.at[task], far_mate)
        yield
        arrive([copy])
        rows_of(z)[...] = (summed(high) + from_far[task].astype(f32)).astype(bf16)
        far_copy = ship(rows_of(z), rows_of(z), far_mate)
        near_copy = ship(rows_of(z), rows_of(z), near_mate)
        spread(z)
        yield
        arrive([far_copy])
        other = low + 2 * (1 - high)
        copy = ship(rows_of(other), rows_of(other), near_mate)
        spread(other)
        yield
        arrive([near_copy, copy])
        spread(1 - low)
        spread(3 - low)
        yield
        arrive(x_copies)
        spot = whole.at[result, pl.ds(h * rows, rows), at(yours, fine)]
        copy = ship(spot, spot, core_mate)
        yield
        arrive(core_copies + [copy])

    def span(h):
        return slice(h * rows, (h + 1) * rows)

    def give_back(h, a, target):
        spots = target.at[pl.ds(h * block, block), at(z, depth)]
        move(back.at[h, a, at(z, block), :], spots)
        return [ship(back.at[h, a, at(q, block), :], spots, {"expert": q}) for q in peers]

    outgoing = []

    def forward(h):
        own[h, 0].wait()
        arrive(incoming[h, 0])
        if h == 0:
            loads["w_in"].wait()
        yield from reduce(h, 0, h, dot(cols[h, 0], w_in[...], ((1,), (0,))))
        if h == 0:
            loads["first"].wait()
            loads["second"].wait()
            gather_gates()
        for j in range(local):
            lanes = slice(j * width, (j + 1) * width)
            active = jnp.maximum(dot(whole[0, span(h), :], first[j], ((1,), (0,))), 0.0)
            scaled = share[h, :, lanes] * active
            hidden[span(h), lanes] = (scaled * active).astype(bf16)
            twice[h, :, lanes] = 2.0 * scaled
        yield from reduce(
            2 * CHUNKS + h, 2, h, dot(hidden[span(h), :], second[...], ((1,), (0,)))
        )
        back[h, 0] = dot(whole[2, span(h), :], w_out[...], ((1,), (1,))).astype(bf16)
        outgoing.extend(give_back(h, 0, mixed_out))

    def backward(h):
        own[h, 1].wait()
        arrive(incoming[h, 1])
        if h == 0:
            loads["w_out"].wait()
        yield from reduce(CHUNKS + h, 1, h, dot(cols[h, 1], w_out[...], ((1,), (0,))))
        slope[span(h), :] = (
            dot(whole[1, span(h), :], second[...], ((1,), (1,))) * twice[h]
        ).astype(bf16)
        value = dot(slope[span(h), 0:width], first[0], ((1,), (1,)))
        for j in range(1, local):
            lanes = slice(j * width, (j + 1) * width)
            value = value + dot(slope[span(h), lanes], first[j], ((1,), (1,)))
        yield from reduce(3 * CHUNKS + h, 3, h, value)
        back[h, 1] = dot(whole[3, span(h), :], w_in[...], ((1,), (1,))).astype(bf16)
        outgoing.extend(give_back(h, 1, grad_tokens_out))

    def weights():
        g_second[...] = dot(hidden[...], whole[1], ((0,), (0,))).astype(bf16)
        move(g_second, grad_second_out)
        yield
        for j in range(local):
            lanes = slice(j * width, (j + 1) * width)
            g_first[j] = dot(whole[0], slope[:, lanes], ((0,), (0,))).astype(bf16)
        move(g_first, grad_first_out)

    chains = []
    for h in range(CHUNKS):
        chains += [(STAGGER * len(chains), forward(h))]
        chains += [(STAGGER * len(chains), backward(h))]
    chains.append((chains[-1][0] + 9, weights()))
    turn = 0
    while chains:
        for start, chain in list(chains):
            if turn >= start:
                try:
                    next(chain)
                except StopIteration:
                    chains.remove((start, chain))
        turn += 1

    def column(a):
        return jnp.concatenate([cols[h, a] for h in range(CHUNKS)], axis=0)

    g_w_out[...] = dot(column(1), whole[2], ((0,), (0,)))
    move(g_w_out, grad_w_out_out)
    g_w_in[...] = dot(column(0), whole[3], ((0,), (0,)))
    move(g_w_in, grad_w_in_out)
    arrive(outgoing)
    for copy in remote:
        copy.wait_send()
    for copy in near[2 * CHUNKS + 5 :]:
        copy.wait()


def settle_kernel(count, *refs):
    sources, targets, held, sems = refs[:count], refs[count : 2 * count], refs[2 * count : -1], refs[-1]
    loads = [
        pltpu.make_async_copy(sources[i], held[i], sems.at[0, i]) for i in range(count)
    ]
    stores = [
        pltpu.make_async_copy(held[i], targets[i], sems.at[1, i]) for i in range(count)
    ]
    for copy in loads:
        copy.start()
    for load, store in zip(loads, stores):
        load.wait()
        store.start()
    for copy in stores:
        copy.wait()


def settle(*arrays):
    count = len(arrays)
    return pl.pallas_call(
        functools.partial(settle_kernel, count),
        out_shape=[jax.ShapeDtypeStruct(a.shape, a.dtype) for a in arrays],
        in_specs=[pl.BlockSpec(memory_space=pl.ANY)] * count,
        out_specs=[pl.BlockSpec(memory_space=pl.ANY)] * count,
        scratch_shapes=[pltpu.VMEM(a.shape, a.dtype) for a in arrays]
        + [pltpu.SemaphoreType.DMA((2, count))],
        compiler_params=pltpu.CompilerParams(vmem_limit_bytes=56 * 1024 * 1024),
        name="settle",
    )(*arrays)


def fused_layer(tokens, routes, gates, w_in, w_out, w_first, w_second, out_grad):
    bf16, f32 = jnp.bfloat16, jnp.float32
    shards = lax.axis_size("expert")
    local, latent, width = w_first.shape
    count, depth = tokens.shape[0], w_in.shape[0]
    rows, block = count * shards // CHUNKS, count // CHUNKS
    tasks, ships, moves = 4 * CHUNKS, 4 * CHUNKS * 18, 8 * CHUNKS + 16
    ships += (4 * CHUNKS + 1) * (shards - 1)
    experts = jnp.arange(local * shards, dtype=jnp.int32)[:, None, None]
    named = jnp.sum(jnp.where(routes.T[None] == experts, gates.T[None], 0.0), axis=1)
    both = local * width
    shape = jax.ShapeDtypeStruct
    outs = pl.pallas_call(
        functools.partial(fused_kernel, shards),
        out_shape=[
            shape(tokens.shape, bf16),
            shape(tokens.shape, bf16),
            shape(w_in.shape, f32),
            shape(w_out.shape, f32),
            shape(w_first.shape, bf16),
            shape((both, latent), bf16),
        ],
        in_specs=[pl.BlockSpec(memory_space=pltpu.VMEM)] + [pl.BlockSpec(memory_space=pl.ANY)] * 6,
        out_specs=[pl.BlockSpec(memory_space=pl.ANY)] * 6,
        scratch_shapes=[
            pltpu.VMEM(w_in.shape, bf16),
            pltpu.VMEM(w_out.shape, bf16),
            pltpu.VMEM(w_first.shape, bf16),
            pltpu.VMEM((both, latent), bf16),
            pltpu.VMEM((CHUNKS, 2, rows, depth), bf16),
            pltpu.VMEM((shards,) + named.shape, f32),
            pltpu.VMEM((CHUNKS, rows, both), f32),
            pltpu.VMEM((CHUNKS, rows, both), f32),
            pltpu.VMEM((CHUNKS * rows, both), bf16),
            pltpu.VMEM((CHUNKS * rows, both), bf16),
            pltpu.VMEM((tasks, 2, 2, block, latent), bf16),
            pltpu.VMEM((tasks, 2, 2, block, latent // 2), bf16),
            pltpu.VMEM((tasks, 2, 2, block, latent // 4), bf16),
            pltpu.VMEM((tasks, 2, 2, block, latent // 4), bf16),
            pltpu.VMEM((tasks, 2, block, latent // 4), bf16),
            pltpu.VMEM((tasks, 2, block, latent // 4), bf16),
            pltpu.VMEM((tasks, block, latent // 4), bf16),
            pltpu.VMEM((tasks, block, latent // 4), bf16),
            pltpu.VMEM((4, CHUNKS * rows, latent), bf16),
            pltpu.VMEM((CHUNKS, 2, rows, depth), bf16),
            pltpu.VMEM(w_in.shape, f32),
            pltpu.VMEM(w_out.shape, f32),
            pltpu.VMEM(w_first.shape, bf16),
            pltpu.VMEM((both, latent), bf16),
            pltpu.SemaphoreType.DMA((ships,)),
            pltpu.SemaphoreType.DMA((ships,)),
            pltpu.SemaphoreType.DMA((moves,)),
        ],
        compiler_params=pltpu.CompilerParams(
            collective_id=0, has_side_effects=True, vmem_limit_bytes=56 * 1024 * 1024
        ),
        name="fused_layer",
    )(named, tokens, out_grad, w_in, w_out, w_first, w_second.reshape(both, latent))
    outs = settle(*outs)
    return (*outs[:5], outs[5].reshape(w_second.shape))


def layer(*args):
    tokens, routes, w_first = args[0], args[1], args[5]
    shards = lax.axis_size("expert")
    count, experts = tokens.shape[0], w_first.shape[0] * shards
    if 5 * count * routes.shape[1] // (2 * experts) >= count and lax.axis_size("dp") == 4 == shards:
        return fused_layer(*args)
    return body(*args)


def solution(mesh):
    placed = (
        P(("groups", "expert"), "dp"),
        P(("groups", "expert"), None),
        P(("groups", "expert"), None),
        P(("dp", "expert"), None),
        P(("dp", "expert"), None),
        P("expert", None, "dp"),
        P("expert", "dp", None),
        P(("groups", "expert"), "dp"),
    )
    return jax.shard_map(
        layer,
        mesh=mesh,
        in_specs=placed,
        out_specs=(
            P(("groups", "expert"), "dp"),
            P(("groups", "expert"), "dp"),
            P(("groups", "dp", "expert"), None),
            P(("groups", "dp", "expert"), None),
            P(("groups", "expert"), None, "dp"),
            P(("groups", "expert"), "dp", None),
        ),
        check_vma=False,
    )
```
